512 devices in a mesh: replica: 8 (over z), fsdp: 64 (over y, x, core).
Axes of the slice: x: 4, y: 8, z: 8, core: 2. Of those that a mesh axis runs over, the one named last changes fastest.
Arguments:
- grad_partials: float32 [8, 5120, 7168], P('replica', 'fsdp'), may hold values from -3300 to 3300
- momentum: float32 [5120, 7168], P('fsdp', 'replica'), may hold values from -4600 to 4600
Outputs:
- update: float32 [5120, 7168], P('fsdp', 'replica')
- momentum_next: float32 [5120, 7168], P('fsdp', 'replica')
The draws below stay inside these ranges and needn't reach their ends.
All inputs are finite; a program needn't handle non-finite values.
Results may differ from the reference program's by a relative error of at most 0.0003.
Values sent between devices are 32-bit elements; how exact they have to be, the bound alone decides.
No kernel may reach another device: no remote copies, remote signals or barrier semaphores. Data moves between devices by JAX's collectives and lax.ppermute only.
A program may use at most 64 MiB of HBM per device.

```python
import math
import jax
import jax.numpy as jnp
from jax import lax

COLS = 5120
HEAD_DIM = 128
HEADS = 56
ITERS = 5
N_REPLICA = 8


def shared_scales(key):
    row_key, col_key = jax.random.split(key)
    row_scale = jnp.exp(jax.random.uniform(row_key, (1, HEADS * HEAD_DIM), jnp.float32, 0.0, math.log(10.0)))
    ramp = jnp.arange(COLS, dtype=jnp.float32) / COLS
    col_scale = jnp.exp(jax.random.uniform(col_key, (COLS, 1), jnp.float32, 0.0, math.log(10.0)))
    col_scale = col_scale * jnp.exp(math.log(3.0) * ramp)[:, None]
    return (row_scale, col_scale)


def draw_grad_partials(key, part):
    row_scale, col_scale = shared_scales(key)
    key = jax.random.fold_in(key, 5)
    own_key = jax.random.fold_in(key, 0)
    normal_vals = jnp.clip(jax.random.normal(own_key, (N_REPLICA, COLS, HEADS * HEAD_DIM), jnp.float32), -4.0, 4.0)
    values = normal_vals * (row_scale * col_scale)[None]
    return values.astype(jnp.float32)


def draw_momentum(key, part):
    row_scale, col_scale = shared_scales(key)
    key = jax.random.fold_in(key, 9)
    values = jnp.clip(jax.random.normal(key, (COLS, HEADS * HEAD_DIM), jnp.float32), -4.0, 4.0)
    values = 3.0 * values * row_scale * col_scale
    return values.astype(jnp.float32)


def setup_inputs(seed: int = 0) -> dict:
    key_list = jax.random.split(jax.random.key(seed), 3)
    grad_partials = draw_grad_partials(jax.random.fold_in(key_list[2], 71), 0)
    momentum = draw_momentum(jax.random.fold_in(key_list[2], 71), 0)
    return dict(grad_partials=grad_partials, momentum=momentum)


quintic_a = 3.4445
quintic_b = -4.775
quintic_c = 2.0315
beta_decay = 0.95
norm_eps = 1e-07
highest = lax.Precision.HIGHEST

def newton_schulz(slices):
    total = jnp.sum(slices * slices)
    current = slices / (jnp.sqrt(total) + norm_eps)
    for iteration in range(ITERS):
        square = jnp.dot(current.T, current, precision=highest, preferred_element_type=jnp.float32)
        polynomial = quintic_b * square + quintic_c * jnp.dot(square, square, precision=highest, preferred_element_type=jnp.float32)
        current = quintic_a * current + jnp.dot(current, polynomial, precision=highest, preferred_element_type=jnp.float32)
    return current

def reference(grad_partials, momentum):
    grad_sum = lax.optimization_barrier(jnp.sum(grad_partials, axis=0))
    momentum_next = beta_decay * momentum + grad_sum
    blended = grad_sum + beta_decay * momentum_next
    per_head = jnp.transpose(blended.reshape(COLS, HEADS, HEAD_DIM), (1, 0, 2))
    orthogonal = lax.map(newton_schulz, per_head)
    factor = 0.2 * math.sqrt(max(HEAD_DIM, COLS))
    update = factor * jnp.transpose(orthogonal, (1, 0, 2)).reshape(COLS, HEADS * HEAD_DIM)
    return (update, momentum_next)
```

```python
import functools
import math

import jax
import jax.numpy as jnp
from jax import lax
from jax.experimental import pallas as pl
from jax.experimental.pallas import tpu as pltpu
from jax.sharding import Mesh, PartitionSpec as P

COLS = 5120
HEAD_DIM = 128
HALF = HEAD_DIM // 2
PACKED = HALF + 8
ITERS = 5

quintic_a = 3.4445
quintic_b = -4.775
quintic_c = 2.0315
beta_decay = 0.95
norm_eps = 1e-07
highest = lax.Precision.HIGHEST

COLUMN_AXES = ("y", "x", "core")
OWNERS = ("x", "core")


def iotas(rows):
    shape = (rows, HEAD_DIM)
    return lax.broadcasted_iota(jnp.int32, shape, 0), lax.broadcasted_iota(jnp.int32, shape, 1)


def pack(full):
    i, j = iotas(HALF)
    body = jnp.where(j > i, full[:HALF], pltpu.roll(full[HALF:], HALF, 1))
    i, j = iotas(HEAD_DIM)
    diagonal = jnp.sum(jnp.where(i == j, full, 0.0), axis=0, keepdims=True)
    return body, jnp.broadcast_to(diagonal, (8, HEAD_DIM))


def unpack(packed):
    i, j = iotas(HALF)
    body = packed[:HALF]
    top = jnp.where(j > i, body, 0.0)
    bottom = pltpu.roll(jnp.where(j < i, body, 0.0), HALF, 1)
    triangle = jnp.concatenate([top, bottom], axis=0)
    i, j = iotas(HEAD_DIM)
    diagonal = jnp.broadcast_to(packed[HALF : HALF + 1], (HEAD_DIM, HEAD_DIM))
    return jnp.where(i == j, diagonal, triangle + triangle.T)


def dot(a, b, contract=((1,), (0,))):
    return lax.dot_general(
        a, b, (contract, ((), ())), precision=highest, preferred_element_type=jnp.float32
    )


def momentum_and_gram(own_ref, right_ref, left_ref, momentum_ref, next_ref, blended_ref, gram_ref):
    grad_sum = own_ref[...] + right_ref[...] + left_ref[...]
    momentum_next = beta_decay * momentum_ref[...] + grad_sum
    next_ref[...] = momentum_next
    blended = grad_sum + beta_decay * momentum_next
    blended_ref[...] = blended
    heads = blended.shape[1] // HEAD_DIM
    for h in range(gram_ref.shape[0]):
        if h < heads:
            part = blended[:, h * HEAD_DIM : (h + 1) * HEAD_DIM]
            body, diagonal = pack(dot(part, part, ((0,), (0,))))
            gram_ref[h, :HALF] = body
            gram_ref[h, HALF:] = diagonal
        else:
            gram_ref[h] = jnp.zeros_like(gram_ref[h])


def newton_schulz(parts_ref, out_ref):
    packed = jnp.sum(parts_ref[...], axis=0)
    total = jnp.sum(packed[HALF : HALF + 1])
    scale = 1.0 / (jnp.sqrt(total) + norm_eps)
    square = unpack(packed) * scale * scale
    i, j = iotas(HEAD_DIM)
    eye = jnp.where(i == j, quintic_a, 0.0)
    product = None
    for iteration in range(ITERS):
        polynomial = eye + quintic_b * square + quintic_c * dot(square, square)
        product = polynomial if product is None else dot(product, polynomial)
        if iteration < ITERS - 1:
            square = dot(dot(square, polynomial), polynomial)
    factor = 0.2 * math.sqrt(max(HEAD_DIM, COLS))
    body, diagonal = pack(product * (factor * scale))
    out_ref[:HALF] = body
    out_ref[HALF:] = diagonal


def apply(blended_ref, product_ref, out_ref):
    for h in range(out_ref.shape[1] // HEAD_DIM):
        cols = slice(h * HEAD_DIM, (h + 1) * HEAD_DIM)
        out_ref[:, cols] = dot(blended_ref[:, cols], unpack(product_ref[h]))


def call(body, out_shape, *args):
    return pl.pallas_call(
        body,
        out_shape=out_shape,
        compiler_params=pltpu.CompilerParams(vmem_limit_bytes=32 * 1024 * 1024),
    )(*args)


def f32(*shape):
    return jax.ShapeDtypeStruct(shape, jnp.float32)


def replica_sums(grad):
    size, me = lax.axis_size("replica"), lax.axis_index("replica")
    width = grad.shape[1] // size

    def chunk(k):
        return lax.dynamic_slice(grad, (0, lax.rem(me + k, size) * width), (grad.shape[0], width))

    def send(value, step):
        return lax.ppermute(value, "replica", [(i, (i + step) % size) for i in range(size)])

    far, half = chunk(size // 2), width // 256 * 128
    right = send(far[:, :half], 1)
    left = send(far[:, half:], -1)
    near_right, near_left = chunk(3), chunk(5)
    right = jnp.concatenate([near_right[:, :half] + right, near_right[:, half:]], axis=1)
    left = jnp.concatenate([near_left[:, :half], near_left[:, half:] + left], axis=1)
    for k in (2, 1, 0):
        right, left = send(right, 1), send(left, -1)
        if k:
            right, left = chunk(k) + right, chunk(size - k) + left
    return chunk(0), right, left


def on_device(grad_partials, momentum):
    own, right, left = replica_sums(grad_partials[0])
    cols, rows = momentum.shape
    heads = rows // HEAD_DIM
    owners = lax.axis_size(OWNERS)
    momentum_next, blended, gram = call(
        momentum_and_gram,
        (f32(cols, rows), f32(cols, rows), f32(owners, PACKED, HEAD_DIM)),
        own,
        right,
        left,
        momentum,
    )
    parts = lax.all_to_all(gram, OWNERS, split_axis=0, concat_axis=0, tiled=True)
    part = jnp.sum(parts, axis=0)
    parts = jnp.broadcast_to(part[None], (lax.axis_size("y"), PACKED, HEAD_DIM))
    parts = lax.all_to_all(parts, "y", split_axis=0, concat_axis=0, tiled=True)
    product = call(newton_schulz, f32(PACKED, HEAD_DIM), parts)
    products = jnp.broadcast_to(product[None], (owners, PACKED, HEAD_DIM))
    products = lax.all_to_all(products, OWNERS, split_axis=0, concat_axis=0, tiled=True)
    update = call(apply, f32(cols, rows), blended, products)
    return update, momentum_next


def solution(mesh):
    fine = Mesh(mesh.devices.reshape(8, 8, 4, 2), ("replica", *COLUMN_AXES))
    return jax.shard_map(
        on_device,
        mesh=fine,
        in_specs=(P("replica", COLUMN_AXES, None), P(COLUMN_AXES, "replica")),
        out_specs=(P(COLUMN_AXES, "replica"), P(COLUMN_AXES, "replica")),
        check_vma=False,
    )
```

```python
import functools
import math

import jax
import jax.numpy as jnp
from jax import lax
from jax.experimental import pallas as pl
from jax.experimental.pallas import tpu as pltpu
from jax.sharding import Mesh, PartitionSpec as P

COLS = 5120
HEAD_DIM = 128
HALF = HEAD_DIM // 2
PACKED = HALF + 8
ITERS = 5

quintic_a = 3.4445
quintic_b = -4.775
quintic_c = 2.0315
beta_decay = 0.95
norm_eps = 1e-07
highest = lax.Precision.HIGHEST

COLUMN_AXES = ("y", "x", "core")
OWNERS = ("x", "core")


def iotas(rows):
    shape = (rows, HEAD_DIM)
    return lax.broadcasted_iota(jnp.int32, shape, 0), lax.broadcasted_iota(jnp.int32, shape, 1)


def pack(full):
    i, j = iotas(HALF)
    body = jnp.where(j > i, full[:HALF], pltpu.roll(full[HALF:], HALF, 1))
    i, j = iotas(HEAD_DIM)
    diagonal = jnp.sum(jnp.where(i == j, full, 0.0), axis=0, keepdims=True)
    return body, jnp.broadcast_to(diagonal, (8, HEAD_DIM))


def unpack(packed):
    i, j = iotas(HALF)
    body = packed[:HALF]
    top = jnp.where(j > i, body, 0.0)
    bottom = pltpu.roll(jnp.where(j < i, body, 0.0), HALF, 1)
    triangle = jnp.concatenate([top, bottom], axis=0)
    i, j = iotas(HEAD_DIM)
    diagonal = jnp.broadcast_to(packed[HALF : HALF + 1], (HEAD_DIM, HEAD_DIM))
    return jnp.where(i == j, diagonal, triangle + triangle.T)


def dot(a, b, contract=((1,), (0,))):
    return lax.dot_general(
        a, b, (contract, ((), ())), precision=highest, preferred_element_type=jnp.float32
    )


def momentum_and_gram(*refs):
    *term_refs, momentum_ref, next_ref, blended_ref, gram_ref = refs
    grad_sum = term_refs[0][...]
    for term_ref in term_refs[1:]:
        grad_sum = grad_sum + term_ref[...]
    momentum_next = beta_decay * momentum_ref[...] + grad_sum
    next_ref[...] = momentum_next
    blended = grad_sum + beta_decay * momentum_next
    blended_ref[...] = blended
    heads = blended.shape[1] // HEAD_DIM
    for h in range(gram_ref.shape[0]):
        if h < heads:
            part = blended[:, h * HEAD_DIM : (h + 1) * HEAD_DIM]
            body, diagonal = pack(dot(part, part, ((0,), (0,))))
            gram_ref[h, :HALF] = body
            gram_ref[h, HALF:] = diagonal
        else:
            gram_ref[h] = jnp.zeros_like(gram_ref[h])


def newton_schulz(parts_ref, out_ref):
    packed = jnp.sum(parts_ref[...], axis=0)
    total = jnp.sum(packed[HALF : HALF + 1])
    scale = 1.0 / (jnp.sqrt(total) + norm_eps)
    square = unpack(packed) * scale * scale
    i, j = iotas(HEAD_DIM)
    eye = jnp.where(i == j, quintic_a, 0.0)
    product = None
    for iteration in range(ITERS):
        polynomial = eye + quintic_b * square + quintic_c * dot(square, square)
        product = polynomial if product is None else dot(product, polynomial)
        if iteration < ITERS - 1:
            square = dot(dot(square, polynomial), polynomial)
    factor = 0.2 * math.sqrt(max(HEAD_DIM, COLS))
    body, diagonal = pack(product * (factor * scale))
    out_ref[:HALF] = body
    out_ref[HALF:] = diagonal


def apply(blended_ref, product_ref, out_ref):
    for h in range(out_ref.shape[1] // HEAD_DIM):
        cols = slice(h * HEAD_DIM, (h + 1) * HEAD_DIM)
        out_ref[:, cols] = dot(blended_ref[:, cols], unpack(product_ref[h]))


def call(body, out_shape, *args):
    return pl.pallas_call(
        body,
        out_shape=out_shape,
        compiler_params=pltpu.CompilerParams(vmem_limit_bytes=32 * 1024 * 1024),
    )(*args)


def f32(*shape):
    return jax.ShapeDtypeStruct(shape, jnp.float32)


def replica_sums(grad):
    size, me = lax.axis_size("replica"), lax.axis_index("replica")
    width = grad.shape[1] // size
    half = width // 256 * 128

    def chunk(k, start=0, stop=width):
        return lax.dynamic_slice(
            grad, (0, lax.rem(me + k + size, size) * width + start), (grad.shape[0], stop - start)
        )

    def send(value, step):
        return lax.ppermute(value, "replica", [(i, (i + step) % size) for i in range(size)])

    far_right, far_left = send(chunk(4, 0, half), 2), send(chunk(4, half), -2)
    next_right, next_left = send(chunk(3), 1), send(chunk(-3), -1)
    right, left = send(chunk(1), 1), send(chunk(-1), -1)
    through_right = chunk(2) + next_right
    through_right = jnp.concatenate([through_right[:, :half] + far_right, through_right[:, half:]], axis=1)
    through_left = chunk(-2) + next_left
    through_left = jnp.concatenate([through_left[:, :half], through_left[:, half:] + far_left], axis=1)
    through_right, through_left = send(through_right, 2), send(through_left, -2)
    return chunk(0), right, left, through_right, through_left


def on_device(grad_partials, momentum):
    terms = replica_sums(grad_partials[0])
    cols, rows = momentum.shape
    heads = rows // HEAD_DIM
    owners = lax.axis_size(OWNERS)
    momentum_next, blended, gram = call(
        momentum_and_gram,
        (f32(cols, rows), f32(cols, rows), f32(owners, PACKED, HEAD_DIM)),
        *terms,
        momentum,
    )
    parts = lax.all_to_all(gram, OWNERS, split_axis=0, concat_axis=0, tiled=True)
    part = jnp.sum(parts, axis=0)
    parts = jnp.broadcast_to(part[None], (lax.axis_size("y"), PACKED, HEAD_DIM))
    parts = lax.all_to_all(parts, "y", split_axis=0, concat_axis=0, tiled=True)
    product = call(newton_schulz, f32(PACKED, HEAD_DIM), parts)
    products = jnp.broadcast_to(product[None], (owners, PACKED, HEAD_DIM))
    products = lax.all_to_all(products, OWNERS, split_axis=0, concat_axis=0, tiled=True)
    update = call(apply, f32(cols, rows), blended, products)
    return update, momentum_next


def solution(mesh):
    fine = Mesh(mesh.devices.reshape(8, 8, 4, 2), ("replica", *COLUMN_AXES))
    return jax.shard_map(
        on_device,
        mesh=fine,
        in_specs=(P("replica", COLUMN_AXES, None), P(COLUMN_AXES, "replica")),
        out_specs=(P(COLUMN_AXES, "replica"), P(COLUMN_AXES, "replica")),
        check_vma=False,
    )
```

```python
import functools
import math

import jax
import jax.numpy as jnp
from jax import lax
from jax.experimental import pallas as pl
from jax.experimental.pallas import tpu as pltpu
from jax.sharding import Mesh, PartitionSpec as P

COLS = 5120
HEAD_DIM = 128
HALF = HEAD_DIM // 2
PACKED = HALF + 8
ITERS = 5

quintic_a = 3.4445
quintic_b = -4.775
quintic_c = 2.0315
beta_decay = 0.95
norm_eps = 1e-07
highest = lax.Precision.HIGHEST

COLUMN_AXES = ("y", "x", "core")
OWNERS = ("x", "core")


def iotas(rows):
    shape = (rows, HEAD_DIM)
    return lax.broadcasted_iota(jnp.int32, shape, 0), lax.broadcasted_iota(jnp.int32, shape, 1)


def pack(full):
    i, j = iotas(HALF)
    body = jnp.where(j > i, full[:HALF], pltpu.roll(full[HALF:], HALF, 1))
    i, j = iotas(HEAD_DIM)
    diagonal = jnp.sum(jnp.where(i == j, full, 0.0), axis=0, keepdims=True)
    return body, jnp.broadcast_to(diagonal, (8, HEAD_DIM))


def unpack(packed):
    i, j = iotas(HALF)
    body = packed[:HALF]
    top = jnp.where(j > i, body, 0.0)
    bottom = pltpu.roll(jnp.where(j < i, body, 0.0), HALF, 1)
    triangle = jnp.concatenate([top, bottom], axis=0)
    i, j = iotas(HEAD_DIM)
    diagonal = jnp.broadcast_to(packed[HALF : HALF + 1], (HEAD_DIM, HEAD_DIM))
    return jnp.where(i == j, diagonal, triangle + triangle.T)


def dot(a, b, contract=((1,), (0,))):
    return lax.dot_general(
        a, b, (contract, ((), ())), precision=highest, preferred_element_type=jnp.float32
    )


def momentum_and_gram(*refs):
    *term_refs, momentum_ref, next_ref, blended_ref, gram_ref = refs
    grad_sum = term_refs[0][...]
    for term_ref in term_refs[1:]:
        grad_sum = grad_sum + term_ref[...]
    momentum_next = beta_decay * momentum_ref[...] + grad_sum
    next_ref[...] = momentum_next
    blended = grad_sum + beta_decay * momentum_next
    blended_ref[...] = blended
    heads = blended.shape[1] // HEAD_DIM
    for h in range(gram_ref.shape[0]):
        if h < heads:
            part = blended[:, h * HEAD_DIM : (h + 1) * HEAD_DIM]
            body, diagonal = pack(dot(part, part, ((0,), (0,))))
            gram_ref[h, :HALF] = body
            gram_ref[h, HALF:] = diagonal
        else:
            gram_ref[h] = jnp.zeros_like(gram_ref[h])


def newton_schulz(parts_ref, out_ref):
    packed = jnp.sum(parts_ref[...], axis=0)
    total = jnp.sum(packed[HALF : HALF + 1])
    scale = 1.0 / (jnp.sqrt(total) + norm_eps)
    square = unpack(packed) * scale * scale
    i, j = iotas(HEAD_DIM)
    eye = jnp.where(i == j, quintic_a, 0.0)
    product = None
    for iteration in range(ITERS):
        polynomial = eye + quintic_b * square + quintic_c * dot(square, square)
        product = polynomial if product is None else dot(product, polynomial)
        if iteration < ITERS - 1:
            square = dot(dot(square, polynomial), polynomial)
    factor = 0.2 * math.sqrt(max(HEAD_DIM, COLS))
    body, diagonal = pack(product * (factor * scale))
    out_ref[:HALF] = body
    out_ref[HALF:] = diagonal


def apply(blended_ref, product_ref, out_ref):
    for h in range(out_ref.shape[1] // HEAD_DIM):
        cols = slice(h * HEAD_DIM, (h + 1) * HEAD_DIM)
        out_ref[:, cols] = dot(blended_ref[:, cols], unpack(product_ref[h]))


def call(body, out_shape, *args):
    return pl.pallas_call(
        body,
        out_shape=out_shape,
        compiler_params=pltpu.CompilerParams(vmem_limit_bytes=32 * 1024 * 1024),
    )(*args)


def f32(*shape):
    return jax.ShapeDtypeStruct(shape, jnp.float32)


def replica_sums(grad):
    size, me, core = lax.axis_size("replica"), lax.axis_index("replica"), lax.axis_index("core")
    width = grad.shape[1] // size
    toward = 1 - 2 * lax.rem(me + core, 2)

    def chunk(k):
        return lax.dynamic_slice(
            grad, (0, lax.rem(me + toward * k + size, size) * width), (grad.shape[0], width)
        )

    def send(value, distance):
        pairs = []
        for i in range(size):
            for c in range(2):
                j = (i + distance * (1 - 2 * ((i + c) % 2))) % size
                pairs.append((2 * i + c, 2 * j + c))
        return lax.ppermute(value, ("replica", "core"), pairs)

    partner = [send(chunk(k), 1) for k in (4, 3, 2, 1)]
    others = [send(chunk(-k) + part, -k) for k, part in zip((3, 2, 1), partner)]
    return chunk(0), partner[3], *others


def on_device(grad_partials, momentum):
    terms = replica_sums(grad_partials[0])
    cols, rows = momentum.shape
    heads = rows // HEAD_DIM
    owners = lax.axis_size(OWNERS)
    momentum_next, blended, gram = call(
        momentum_and_gram,
        (f32(cols, rows), f32(cols, rows), f32(owners, PACKED, HEAD_DIM)),
        *terms,
        momentum,
    )
    parts = lax.all_to_all(gram, OWNERS, split_axis=0, concat_axis=0, tiled=True)
    part = jnp.sum(parts, axis=0)
    parts = jnp.broadcast_to(part[None], (lax.axis_size("y"), PACKED, HEAD_DIM))
    parts = lax.all_to_all(parts, "y", split_axis=0, concat_axis=0, tiled=True)
    product = call(newton_schulz, f32(PACKED, HEAD_DIM), parts)
    products = jnp.broadcast_to(product[None], (owners, PACKED, HEAD_DIM))
    products = lax.all_to_all(products, OWNERS, split_axis=0, concat_axis=0, tiled=True)
    update = call(apply, f32(cols, rows), blended, products)
    return update, momentum_next


def solution(mesh):
    fine = Mesh(mesh.devices.reshape(8, 8, 4, 2), ("replica", *COLUMN_AXES))
    return jax.shard_map(
        on_device,
        mesh=fine,
        in_specs=(P("replica", COLUMN_AXES, None), P(COLUMN_AXES, "replica")),
        out_specs=(P(COLUMN_AXES, "replica"), P(COLUMN_AXES, "replica")),
        check_vma=False,
    )
```

```python
import functools
import math

import jax
import jax.numpy as jnp
from jax import lax
from jax.experimental import pallas as pl
from jax.experimental.pallas import tpu as pltpu
from jax.sharding import Mesh, PartitionSpec as P

COLS = 5120
HEAD_DIM = 128
HALF = HEAD_DIM // 2
PACKED = HALF + 8
ITERS = 5

quintic_a = 3.4445
quintic_b = -4.775
quintic_c = 2.0315
beta_decay = 0.95
norm_eps = 1e-07
highest = lax.Precision.HIGHEST

COLUMN_AXES = ("y", "x", "core")
OWNERS = ("x", "core")


def iotas(rows):
    shape = (rows, HEAD_DIM)
    return lax.broadcasted_iota(jnp.int32, shape, 0), lax.broadcasted_iota(jnp.int32, shape, 1)


def pack(full):
    i, j = iotas(HALF)
    body = jnp.where(j > i, full[:HALF], pltpu.roll(full[HALF:], HALF, 1))
    i, j = iotas(HEAD_DIM)
    diagonal = jnp.sum(jnp.where(i == j, full, 0.0), axis=0, keepdims=True)
    return body, jnp.broadcast_to(diagonal, (8, HEAD_DIM))


def unpack(packed):
    i, j = iotas(HALF)
    body = packed[:HALF]
    top = jnp.where(j > i, body, 0.0)
    bottom = pltpu.roll(jnp.where(j < i, body, 0.0), HALF, 1)
    triangle = jnp.concatenate([top, bottom], axis=0)
    i, j = iotas(HEAD_DIM)
    diagonal = jnp.broadcast_to(packed[HALF : HALF + 1], (HEAD_DIM, HEAD_DIM))
    return jnp.where(i == j, diagonal, triangle + triangle.T)


def dot(a, b, contract=((1,), (0,))):
    return lax.dot_general(
        a, b, (contract, ((), ())), precision=highest, preferred_element_type=jnp.float32
    )


def momentum_and_gram(*refs):
    *term_refs, momentum_ref, next_ref, blended_ref, gram_ref = refs
    grad_sum = term_refs[0][...]
    for term_ref in term_refs[1:]:
        grad_sum = grad_sum + term_ref[...]
    momentum_next = beta_decay * momentum_ref[...] + grad_sum
    next_ref[...] = momentum_next
    blended = grad_sum + beta_decay * momentum_next
    blended_ref[...] = blended
    heads = blended.shape[1] // HEAD_DIM
    for h in range(gram_ref.shape[0]):
        if h < heads:
            part = blended[:, h * HEAD_DIM : (h + 1) * HEAD_DIM]
            body, diagonal = pack(dot(part, part, ((0,), (0,))))
            gram_ref[h, :HALF] = body
            gram_ref[h, HALF:] = diagonal
        else:
            gram_ref[h] = jnp.zeros_like(gram_ref[h])


def newton_schulz(parts_ref, out_ref):
    packed = jnp.sum(parts_ref[...], axis=0)
    total = jnp.sum(packed[HALF : HALF + 1])
    scale = 1.0 / (jnp.sqrt(total) + norm_eps)
    square = unpack(packed) * scale * scale
    i, j = iotas(HEAD_DIM)
    eye = jnp.where(i == j, quintic_a, 0.0)
    product = None
    for iteration in range(ITERS):
        polynomial = eye + quintic_b * square + quintic_c * dot(square, square)
        product = polynomial if product is None else dot(product, polynomial)
        if iteration < ITERS - 1:
            square = dot(dot(square, polynomial), polynomial)
    factor = 0.2 * math.sqrt(max(HEAD_DIM, COLS))
    body, diagonal = pack(product * (factor * scale))
    out_ref[:HALF] = body
    out_ref[HALF:] = diagonal


def apply(blended_ref, product_ref, out_ref):
    for h in range(out_ref.shape[1] // HEAD_DIM):
        cols = slice(h * HEAD_DIM, (h + 1) * HEAD_DIM)
        out_ref[:, cols] = dot(blended_ref[:, cols], unpack(product_ref[h]))


def call(body, out_shape, *args):
    return pl.pallas_call(
        body,
        out_shape=out_shape,
        compiler_params=pltpu.CompilerParams(vmem_limit_bytes=32 * 1024 * 1024),
    )(*args)


def f32(*shape):
    return jax.ShapeDtypeStruct(shape, jnp.float32)


def replica_sums(grad):
    size, me, core = lax.axis_size("replica"), lax.axis_index("replica"), lax.axis_index("core")
    width = grad.shape[1] // size
    toward = 1 - 2 * lax.rem(me + core, 2)

    def chunk(k):
        return lax.dynamic_slice(
            grad, (0, lax.rem(me + toward * k + size, size) * width), (grad.shape[0], width)
        )

    def send(value, distance):
        pairs = []
        for i in range(size):
            for c in range(2):
                j = (i + distance * (1 - 2 * ((i + c) % 2))) % size
                pairs.append((2 * i + c, 2 * j + c))
        return lax.ppermute(value, ("replica", "core"), pairs)

    offsets = (4, 3, 2, 1, -3, -2, -1, 0)
    chunks = dict(zip(offsets, lax.optimization_barrier(tuple(chunk(k) for k in offsets))))
    fourth, third, second = (send(chunks[k], 1) for k in (4, 3, 2))
    relayed = send(chunks[-3] + fourth, -2)
    partner = send(chunks[1], 1)
    from_second = send(chunks[-2] + third, -2)
    from_first = send(chunks[-1] + second + relayed, -1)
    return chunks[0], partner, from_second, from_first


def on_device(grad_partials, momentum):
    terms = replica_sums(grad_partials[0])
    cols, rows = momentum.shape
    heads = rows // HEAD_DIM
    owners = lax.axis_size(OWNERS)
    momentum_next, blended, gram = call(
        momentum_and_gram,
        (f32(cols, rows), f32(cols, rows), f32(owners, PACKED, HEAD_DIM)),
        *terms,
        momentum,
    )
    parts = lax.all_to_all(gram, OWNERS, split_axis=0, concat_axis=0, tiled=True)
    part = jnp.sum(parts, axis=0)
    parts = jnp.broadcast_to(part[None], (lax.axis_size("y"), PACKED, HEAD_DIM))
    parts = lax.all_to_all(parts, "y", split_axis=0, concat_axis=0, tiled=True)
    product = call(newton_schulz, f32(PACKED, HEAD_DIM), parts)
    products = jnp.broadcast_to(product[None], (owners, PACKED, HEAD_DIM))
    products = lax.all_to_all(products, OWNERS, split_axis=0, concat_axis=0, tiled=True)
    update = call(apply, f32(cols, rows), blended, products)
    return update, momentum_next


def solution(mesh):
    fine = Mesh(mesh.devices.reshape(8, 8, 4, 2), ("replica", *COLUMN_AXES))
    return jax.shard_map(
        on_device,
        mesh=fine,
        in_specs=(P("replica", COLUMN_AXES, None), P(COLUMN_AXES, "replica")),
        out_specs=(P(COLUMN_AXES, "replica"), P(COLUMN_AXES, "replica")),
        check_vma=False,
    )
```

```python
import functools
import math

import jax
import jax.numpy as jnp
from jax import lax
from jax.experimental import pallas as pl
from jax.experimental.pallas import tpu as pltpu
from jax.sharding import Mesh, PartitionSpec as P

COLS = 5120
HEAD_DIM = 128
HALF = HEAD_DIM // 2
PACKED = HALF + 8
ITERS = 5
VMEM = 32 * 1024 * 1024

quintic_a = 3.4445
quintic_b = -4.775
quintic_c = 2.0315
beta_decay = 0.95
norm_eps = 1e-07
highest = lax.Precision.HIGHEST

COLUMN_AXES = ("y", "x", "core")
OWNERS = ("x", "core")


def iotas(rows):
    shape = (rows, HEAD_DIM)
    return lax.broadcasted_iota(jnp.int32, shape, 0), lax.broadcasted_iota(jnp.int32, shape, 1)


def pack(full):
    i, j = iotas(HALF)
    body = jnp.where(j > i, full[:HALF], pltpu.roll(full[HALF:], HALF, 1))
    i, j = iotas(HEAD_DIM)
    diagonal = jnp.sum(jnp.where(i == j, full, 0.0), axis=0, keepdims=True)
    return body, jnp.broadcast_to(diagonal, (8, HEAD_DIM))


def unpack(packed):
    i, j = iotas(HALF)
    body = packed[:HALF]
    top = jnp.where(j > i, body, 0.0)
    bottom = pltpu.roll(jnp.where(j < i, body, 0.0), HALF, 1)
    triangle = jnp.concatenate([top, bottom], axis=0)
    i, j = iotas(HEAD_DIM)
    diagonal = jnp.broadcast_to(packed[HALF : HALF + 1], (HEAD_DIM, HEAD_DIM))
    return jnp.where(i == j, diagonal, triangle + triangle.T)


def dot(a, b, contract=((1,), (0,))):
    return lax.dot_general(
        a, b, (contract, ((), ())), precision=highest, preferred_element_type=jnp.float32
    )


def momentum_and_gram(*refs):
    *term_refs, momentum_ref, next_ref, blended_ref, gram_ref = refs
    grad_sum = term_refs[0][...]
    for term_ref in term_refs[1:]:
        grad_sum = grad_sum + term_ref[...]
    momentum_next = beta_decay * momentum_ref[...] + grad_sum
    next_ref[...] = momentum_next
    blended = grad_sum + beta_decay * momentum_next
    blended_ref[...] = blended
    heads = blended.shape[1] // HEAD_DIM
    cores = gram_ref.shape[0]
    for h in range(cores * gram_ref.shape[1]):
        core, x = h % cores, h // cores
        if h < heads:
            part = blended[:, h * HEAD_DIM : (h + 1) * HEAD_DIM]
            body, diagonal = pack(dot(part, part, ((0,), (0,))))
            gram_ref[core, x, :HALF] = body
            gram_ref[core, x, HALF:] = diagonal
        else:
            gram_ref[core, x] = jnp.zeros_like(gram_ref[core, x])


def newton_schulz(parts_ref, next_ref, out_ref, next_out_ref, sem):
    write = pltpu.make_async_copy(next_ref, next_out_ref, sem)
    write.start()
    packed = jnp.sum(parts_ref[...], axis=0)
    total = jnp.sum(packed[HALF : HALF + 1])
    scale = 1.0 / (jnp.sqrt(total) + norm_eps)
    square = unpack(packed) * scale * scale
    i, j = iotas(HEAD_DIM)
    eye = jnp.where(i == j, quintic_a, 0.0)
    product = None
    for iteration in range(ITERS):
        polynomial = eye + quintic_b * square + quintic_c * dot(square, square)
        product = polynomial if product is None else dot(product, polynomial)
        if iteration < ITERS - 1:
            square = dot(dot(square, polynomial), polynomial)
    factor = 0.2 * math.sqrt(max(HEAD_DIM, COLS))
    body, diagonal = pack(product * (factor * scale))
    out_ref[:HALF] = body
    out_ref[HALF:] = diagonal
    write.wait()


def apply(blended_ref, product_ref, out_ref, held, sems):
    writes = []
    for h in range(out_ref.shape[1] // HEAD_DIM):
        cols = slice(h * HEAD_DIM, (h + 1) * HEAD_DIM)
        held[:, cols] = dot(blended_ref[:, cols], unpack(product_ref[h]))
        writes.append(pltpu.make_async_copy(held.at[:, cols], out_ref.at[:, cols], sems.at[h]))
        writes[-1].start()
    for write in writes:
        write.wait()


def call(body, out_shape, *args):
    return pl.pallas_call(
        body,
        out_shape=out_shape,
        compiler_params=pltpu.CompilerParams(vmem_limit_bytes=VMEM),
    )(*args)


def f32(*shape):
    return jax.ShapeDtypeStruct(shape, jnp.float32)


def replica_sums(grad):
    size, me, core = lax.axis_size("replica"), lax.axis_index("replica"), lax.axis_index("core")
    width = grad.shape[1] // size
    toward = 1 - 2 * lax.rem(me + core, 2)

    def chunk(k):
        return lax.dynamic_slice(
            grad, (0, lax.rem(me + toward * k + size, size) * width), (grad.shape[0], width)
        )

    def send(value, distance):
        pairs = []
        for i in range(size):
            for c in range(2):
                j = (i + distance * (1 - 2 * ((i + c) % 2))) % size
                pairs.append((2 * i + c, 2 * j + c))
        return lax.ppermute(value, ("replica", "core"), pairs)

    offsets = (4, 3, 2, 1, -3, -2, -1, 0)
    chunks = dict(zip(offsets, lax.optimization_barrier(tuple(chunk(k) for k in offsets))))
    fourth, third, second = (send(chunks[k], 1) for k in (4, 3, 2))
    relayed = send(chunks[-3] + fourth, -2)
    partner = send(chunks[1], 1)
    from_second = send(chunks[-2] + third, -2)
    from_first = send(chunks[-1] + second + relayed, -1)
    return chunks[0], partner, from_second, from_first


def on_device(grad_partials, momentum):
    terms = replica_sums(grad_partials[0])
    cols, rows = momentum.shape
    heads = rows // HEAD_DIM
    owners = lax.axis_size(OWNERS)
    owner_grid = (lax.axis_size("core"), lax.axis_size("x"))
    momentum_next, blended, gram = call(
        momentum_and_gram,
        (f32(cols, rows), f32(cols, rows), f32(*owner_grid, PACKED, HEAD_DIM)),
        *terms,
        momentum,
    )
    both = lax.all_gather(gram, "core")
    mine = lax.dynamic_index_in_dim(both, lax.axis_index("core"), axis=1, keepdims=False)
    parts = lax.all_to_all(jnp.sum(mine, axis=0), "x", split_axis=0, concat_axis=0, tiled=True)
    part = jnp.sum(parts, axis=0)
    parts = jnp.broadcast_to(part[None], (lax.axis_size("y"), PACKED, HEAD_DIM))
    parts = lax.all_to_all(parts, "y", split_axis=0, concat_axis=0, tiled=True)
    product, momentum_next = pl.pallas_call(
        newton_schulz,
        in_specs=[pl.BlockSpec(memory_space=pltpu.VMEM), pl.BlockSpec(memory_space=pl.ANY)],
        out_specs=[pl.BlockSpec(memory_space=pltpu.VMEM), pl.BlockSpec(memory_space=pl.ANY)],
        out_shape=[f32(PACKED, HEAD_DIM), f32(cols, rows)],
        scratch_shapes=[pltpu.SemaphoreType.DMA],
        compiler_params=pltpu.CompilerParams(vmem_limit_bytes=VMEM),
    )(parts, momentum_next)
    products = jnp.broadcast_to(product[None], (owners, PACKED, HEAD_DIM))
    products = lax.all_to_all(products, OWNERS, split_axis=0, concat_axis=0, tiled=True)
    update = pl.pallas_call(
        apply,
        in_specs=[pl.BlockSpec(memory_space=pltpu.VMEM)] * 2,
        out_specs=pl.BlockSpec(memory_space=pl.ANY),
        out_shape=f32(cols, rows),
        scratch_shapes=[pltpu.VMEM((cols, rows), jnp.float32), pltpu.SemaphoreType.DMA((heads,))],
        compiler_params=pltpu.CompilerParams(vmem_limit_bytes=VMEM),
    )(blended, products)
    return update, momentum_next


def solution(mesh):
    fine = Mesh(mesh.devices.reshape(8, 8, 4, 2), ("replica", *COLUMN_AXES))
    return jax.shard_map(
        on_device,
        mesh=fine,
        in_specs=(P("replica", COLUMN_AXES, None), P(COLUMN_AXES, "replica")),
        out_specs=(P(COLUMN_AXES, "replica"), P(COLUMN_AXES, "replica")),
        check_vma=False,
    )
```

```python
import functools
import math

import jax
import jax.numpy as jnp
from jax import lax
from jax.experimental import pallas as pl
from jax.experimental.pallas import tpu as pltpu
from jax.sharding import Mesh, PartitionSpec as P

COLS = 5120
HEAD_DIM = 128
HALF = HEAD_DIM // 2
PACKED = HALF + 8
ITERS = 5
VMEM = 32 * 1024 * 1024

quintic_a = 3.4445
quintic_b = -4.775
quintic_c = 2.0315
beta_decay = 0.95
norm_eps = 1e-07
highest = lax.Precision.HIGHEST

COLUMN_AXES = ("y", "x", "core")
OWNERS = ("x", "core")


def iotas(rows):
    shape = (rows, HEAD_DIM)
    return lax.broadcasted_iota(jnp.int32, shape, 0), lax.broadcasted_iota(jnp.int32, shape, 1)


def pack(full):
    i, j = iotas(HALF)
    body = jnp.where(j > i, full[:HALF], pltpu.roll(full[HALF:], HALF, 1))
    i, j = iotas(HEAD_DIM)
    diagonal = jnp.sum(jnp.where(i == j, full, 0.0), axis=0, keepdims=True)
    return body, jnp.broadcast_to(diagonal, (8, HEAD_DIM))


def unpack(packed):
    i, j = iotas(HALF)
    body = packed[:HALF]
    top = jnp.where(j > i, body, 0.0)
    bottom = pltpu.roll(jnp.where(j < i, body, 0.0), HALF, 1)
    triangle = jnp.concatenate([top, bottom], axis=0)
    i, j = iotas(HEAD_DIM)
    diagonal = jnp.broadcast_to(packed[HALF : HALF + 1], (HEAD_DIM, HEAD_DIM))
    return jnp.where(i == j, diagonal, triangle + triangle.T)


def dot(a, b, contract=((1,), (0,))):
    return lax.dot_general(
        a, b, (contract, ((), ())), precision=highest, preferred_element_type=jnp.float32
    )


def thirds(value):
    high = value.astype(jnp.bfloat16)
    rest = value - high.astype(jnp.float32)
    middle = rest.astype(jnp.bfloat16)
    return high, middle, (rest - middle.astype(jnp.float32)).astype(jnp.bfloat16)


def joined_dot(a, b):
    a0, a1, a2 = a
    b0, b1, b2 = b
    left = jnp.concatenate([a0, a1, a0, a2, a1, a0], axis=1)
    right = jnp.concatenate([b0, b0, b1, b0, b1, b2], axis=0)
    return lax.dot_general(left, right, (((1,), (0,)), ((), ())), preferred_element_type=jnp.float32)


def momentum_and_gram(*refs):
    *term_refs, momentum_ref, next_ref, blended_ref, gram_ref = refs
    grad_sum = term_refs[0][...]
    for term_ref in term_refs[1:]:
        grad_sum = grad_sum + term_ref[...]
    momentum_next = beta_decay * momentum_ref[...] + grad_sum
    next_ref[...] = momentum_next
    blended = grad_sum + beta_decay * momentum_next
    blended_ref[...] = blended
    heads = blended.shape[1] // HEAD_DIM
    cores = gram_ref.shape[0]
    for h in range(cores * gram_ref.shape[1]):
        core, x = h % cores, h // cores
        if h < heads:
            part = blended[:, h * HEAD_DIM : (h + 1) * HEAD_DIM]
            body, diagonal = pack(dot(part, part, ((0,), (0,))))
            gram_ref[core, x, :HALF] = body
            gram_ref[core, x, HALF:] = diagonal
        else:
            gram_ref[core, x] = jnp.zeros_like(gram_ref[core, x])


def newton_schulz(parts_ref, next_ref, out_ref, next_out_ref, sem):
    write = pltpu.make_async_copy(next_ref, next_out_ref, sem)
    write.start()
    packed = jnp.sum(parts_ref[...], axis=0)
    total = jnp.sum(packed[HALF : HALF + 1])
    scale = 1.0 / (jnp.sqrt(total) + norm_eps)
    square = unpack(packed) * scale * scale
    i, j = iotas(HEAD_DIM)
    eye = jnp.where(i == j, quintic_a, 0.0)
    product = None
    for iteration in range(ITERS):
        terms = thirds(square)
        polynomial = eye + quintic_b * square + quintic_c * joined_dot(terms, terms)
        factors = thirds(polynomial)
        product = polynomial if product is None else joined_dot(thirds(product), factors)
        if iteration < ITERS - 1:
            square = joined_dot(thirds(joined_dot(terms, factors)), factors)
    factor = 0.2 * math.sqrt(max(HEAD_DIM, COLS))
    body, diagonal = pack(product * (factor * scale))
    out_ref[:HALF] = body
    out_ref[HALF:] = diagonal
    write.wait()


def apply(blended_ref, product_ref, out_ref, held, sems):
    writes = []
    for h in range(out_ref.shape[1] // HEAD_DIM):
        cols = slice(h * HEAD_DIM, (h + 1) * HEAD_DIM)
        held[:, cols] = dot(blended_ref[:, cols], unpack(product_ref[h]))
        writes.append(pltpu.make_async_copy(held.at[:, cols], out_ref.at[:, cols], sems.at[h]))
        writes[-1].start()
    for write in writes:
        write.wait()


def call(body, out_shape, *args):
    return pl.pallas_call(
        body,
        out_shape=out_shape,
        compiler_params=pltpu.CompilerParams(vmem_limit_bytes=VMEM),
    )(*args)


def f32(*shape):
    return jax.ShapeDtypeStruct(shape, jnp.float32)


def replica_sums(grad):
    size, me, core = lax.axis_size("replica"), lax.axis_index("replica"), lax.axis_index("core")
    width = grad.shape[1] // size
    toward = 1 - 2 * lax.rem(me + core, 2)

    def chunk(k):
        return lax.dynamic_slice(
            grad, (0, lax.rem(me + toward * k + size, size) * width), (grad.shape[0], width)
        )

    def send(value, distance):
        pairs = []
        for i in range(size):
            for c in range(2):
                j = (i + distance * (1 - 2 * ((i + c) % 2))) % size
                pairs.append((2 * i + c, 2 * j + c))
        return lax.ppermute(value, ("replica", "core"), pairs)

    offsets = (4, 3, 2, 1, -3, -2, -1, 0)
    chunks = dict(zip(offsets, lax.optimization_barrier(tuple(chunk(k) for k in offsets))))
    fourth, third, second = (send(chunks[k], 1) for k in (4, 3, 2))
    relayed = send(chunks[-3] + fourth, -2)
    to_second, chunks[1] = lax.optimization_barrier((chunks[-2] + third, chunks[1]))
    from_second = send(to_second, -2)
    partner = send(chunks[1], 1)
    from_first = send(chunks[-1] + second + relayed, -1)
    return chunks[0], partner, from_second, from_first


def on_device(grad_partials, momentum):
    terms = replica_sums(grad_partials[0])
    cols, rows = momentum.shape
    heads = rows // HEAD_DIM
    owners = lax.axis_size(OWNERS)
    owner_grid = (lax.axis_size("core"), lax.axis_size("x"))
    momentum_next, blended, gram = call(
        momentum_and_gram,
        (f32(cols, rows), f32(cols, rows), f32(*owner_grid, PACKED, HEAD_DIM)),
        *terms,
        momentum,
    )
    both = lax.all_gather(gram, "core")
    mine = lax.dynamic_index_in_dim(both, lax.axis_index("core"), axis=1, keepdims=False)
    parts = lax.all_to_all(jnp.sum(mine, axis=0), "x", split_axis=0, concat_axis=0, tiled=True)
    part = jnp.sum(parts, axis=0)
    parts = jnp.broadcast_to(part[None], (lax.axis_size("y"), PACKED, HEAD_DIM))
    parts = lax.all_to_all(parts, "y", split_axis=0, concat_axis=0, tiled=True)
    product, momentum_next = pl.pallas_call(
        newton_schulz,
        in_specs=[pl.BlockSpec(memory_space=pltpu.VMEM), pl.BlockSpec(memory_space=pl.ANY)],
        out_specs=[pl.BlockSpec(memory_space=pltpu.VMEM), pl.BlockSpec(memory_space=pl.ANY)],
        out_shape=[f32(PACKED, HEAD_DIM), f32(cols, rows)],
        scratch_shapes=[pltpu.SemaphoreType.DMA],
        compiler_params=pltpu.CompilerParams(vmem_limit_bytes=VMEM),
    )(parts, momentum_next)
    products = jnp.broadcast_to(product[None], (owners, PACKED, HEAD_DIM))
    products = lax.all_to_all(products, OWNERS, split_axis=0, concat_axis=0, tiled=True)
    update = pl.pallas_call(
        apply,
        in_specs=[pl.BlockSpec(memory_space=pltpu.VMEM)] * 2,
        out_specs=pl.BlockSpec(memory_space=pl.ANY),
        out_shape=f32(cols, rows),
        scratch_shapes=[pltpu.VMEM((cols, rows), jnp.float32), pltpu.SemaphoreType.DMA((heads,))],
        compiler_params=pltpu.CompilerParams(vmem_limit_bytes=VMEM),
    )(blended, products)
    return update, momentum_next


def solution(mesh):
    fine = Mesh(mesh.devices.reshape(8, 8, 4, 2), ("replica", *COLUMN_AXES))
    return jax.shard_map(
        on_device,
        mesh=fine,
        in_specs=(P("replica", COLUMN_AXES, None), P(COLUMN_AXES, "replica")),
        out_specs=(P(COLUMN_AXES, "replica"), P(COLUMN_AXES, "replica")),
        check_vma=False,
    )
```

```python
import functools
import math

import jax
import jax.numpy as jnp
from jax import lax
from jax.experimental import pallas as pl
from jax.experimental.pallas import tpu as pltpu
from jax.sharding import Mesh, PartitionSpec as P

COLS = 5120
HEAD_DIM = 128
HALF = HEAD_DIM // 2
PACKED = HALF + 8
ITERS = 5
VMEM = 32 * 1024 * 1024

quintic_a = 3.4445
quintic_b = -4.775
quintic_c = 2.0315
beta_decay = 0.95
norm_eps = 1e-07
highest = lax.Precision.HIGHEST

COLUMN_AXES = ("y", "x", "core")
OWNERS = ("x", "core")


def iotas(rows):
    shape = (rows, HEAD_DIM)
    return lax.broadcasted_iota(jnp.int32, shape, 0), lax.broadcasted_iota(jnp.int32, shape, 1)


def pack(full):
    i, j = iotas(HALF)
    body = jnp.where(j > i, full[:HALF], pltpu.roll(full[HALF:], HALF, 1))
    i, j = iotas(HEAD_DIM)
    diagonal = jnp.sum(jnp.where(i == j, full, 0.0), axis=0, keepdims=True)
    return body, jnp.broadcast_to(diagonal, (8, HEAD_DIM))


def unpack(packed):
    i, j = iotas(HALF)
    body = packed[:HALF]
    top = jnp.where(j > i, body, 0.0)
    bottom = pltpu.roll(jnp.where(j < i, body, 0.0), HALF, 1)
    triangle = jnp.concatenate([top, bottom], axis=0)
    i, j = iotas(HEAD_DIM)
    diagonal = jnp.broadcast_to(packed[HALF : HALF + 1], (HEAD_DIM, HEAD_DIM))
    return jnp.where(i == j, diagonal, triangle + triangle.T)


def dot(a, b, contract=((1,), (0,))):
    return lax.dot_general(
        a, b, (contract, ((), ())), precision=highest, preferred_element_type=jnp.float32
    )


def thirds(value):
    high = value.astype(jnp.bfloat16)
    rest = value - high.astype(jnp.float32)
    middle = rest.astype(jnp.bfloat16)
    return high, middle, (rest - middle.astype(jnp.float32)).astype(jnp.bfloat16)


def joined_dot(a, b):
    a0, a1, a2 = a
    b0, b1, b2 = b
    left = jnp.concatenate([a0, a1, a0, a2, a1, a0], axis=1)
    right = jnp.concatenate([b0, b0, b1, b0, b1, b2], axis=0)
    return lax.dot_general(left, right, (((1,), (0,)), ((), ())), preferred_element_type=jnp.float32)


def momentum_and_gram(*refs):
    *term_refs, momentum_ref, next_ref, blended_ref, gram_ref = refs
    grad_sum = term_refs[0][...]
    for term_ref in term_refs[1:]:
        grad_sum = grad_sum + term_ref[...]
    momentum_next = beta_decay * momentum_ref[...] + grad_sum
    next_ref[...] = momentum_next
    blended = grad_sum + beta_decay * momentum_next
    blended_ref[...] = blended
    heads = blended.shape[1] // HEAD_DIM
    cores = gram_ref.shape[0]
    for h in range(cores * gram_ref.shape[1]):
        core, x = h % cores, h // cores
        if h < heads:
            part = blended[:, h * HEAD_DIM : (h + 1) * HEAD_DIM]
            body, diagonal = pack(dot(part, part, ((0,), (0,))))
            gram_ref[core, x, :HALF] = body
            gram_ref[core, x, HALF:] = diagonal
        else:
            gram_ref[core, x] = jnp.zeros_like(gram_ref[core, x])


def newton_schulz(parts_ref, next_ref, out_ref, next_out_ref, sem):
    write = pltpu.make_async_copy(next_ref, next_out_ref, sem)
    write.start()
    packed = jnp.sum(parts_ref[...], axis=0)
    total = jnp.sum(packed[HALF : HALF + 1])
    scale = 1.0 / (jnp.sqrt(total) + norm_eps)
    square = unpack(packed) * scale * scale
    i, j = iotas(HEAD_DIM)
    eye = jnp.where(i == j, quintic_a, 0.0)
    product = None
    for iteration in range(ITERS):
        terms = thirds(square)
        polynomial = eye + quintic_b * square + quintic_c * joined_dot(terms, terms)
        factors = thirds(polynomial)
        product = polynomial if product is None else joined_dot(thirds(product), factors)
        if iteration < ITERS - 1:
            square = joined_dot(thirds(joined_dot(terms, factors)), factors)
            square = 0.5 * (square + square.T)
    factor = 0.2 * math.sqrt(max(HEAD_DIM, COLS))
    body, diagonal = pack(product * (factor * scale))
    out_ref[:HALF] = body
    out_ref[HALF:] = diagonal
    write.wait()


def apply(blended_ref, product_ref, out_ref, held, sems):
    writes = []
    for h in range(out_ref.shape[1] // HEAD_DIM):
        cols = slice(h * HEAD_DIM, (h + 1) * HEAD_DIM)
        held[:, cols] = dot(blended_ref[:, cols], unpack(product_ref[h]))
        writes.append(pltpu.make_async_copy(held.at[:, cols], out_ref.at[:, cols], sems.at[h]))
        writes[-1].start()
    for write in writes:
        write.wait()


def call(body, out_shape, *args):
    return pl.pallas_call(
        body,
        out_shape=out_shape,
        compiler_params=pltpu.CompilerParams(vmem_limit_bytes=VMEM),
    )(*args)


def f32(*shape):
    return jax.ShapeDtypeStruct(shape, jnp.float32)


def replica_sums(grad):
    size, me, core = lax.axis_size("replica"), lax.axis_index("replica"), lax.axis_index("core")
    width = grad.shape[1] // size
    toward = 1 - 2 * lax.rem(me + core, 2)

    def chunk(k):
        return lax.dynamic_slice(
            grad, (0, lax.rem(me + toward * k + size, size) * width), (grad.shape[0], width)
        )

    def send(value, distance):
        pairs = []
        for i in range(size):
            for c in range(2):
                j = (i + distance * (1 - 2 * ((i + c) % 2))) % size
                pairs.append((2 * i + c, 2 * j + c))
        return lax.ppermute(value, ("replica", "core"), pairs)

    offsets = (4, 3, 2, 1, -3, -2, -1, 0)
    chunks = dict(zip(offsets, lax.optimization_barrier(tuple(chunk(k) for k in offsets))))
    fourth, third, second = (send(chunks[k], 1) for k in (4, 3, 2))
    relayed = send(chunks[-3] + fourth, -2)
    to_second, chunks[1] = lax.optimization_barrier((chunks[-2] + third, chunks[1]))
    from_second = send(to_second, -2)
    partner = send(chunks[1], 1)
    from_first = send(chunks[-1] + second + relayed, -1)
    return chunks[0], partner, from_second, from_first


def on_device(grad_partials, momentum):
    terms = replica_sums(grad_partials[0])
    cols, rows = momentum.shape
    heads = rows // HEAD_DIM
    owners = lax.axis_size(OWNERS)
    owner_grid = (lax.axis_size("core"), lax.axis_size("x"))
    momentum_next, blended, gram = call(
        momentum_and_gram,
        (f32(cols, rows), f32(cols, rows), f32(*owner_grid, PACKED, HEAD_DIM)),
        *terms,
        momentum,
    )
    both = lax.all_gather(gram, "core")
    mine = lax.dynamic_index_in_dim(both, lax.axis_index("core"), axis=1, keepdims=False)
    parts = lax.all_to_all(jnp.sum(mine, axis=0), "x", split_axis=0, concat_axis=0, tiled=True)
    part = jnp.sum(parts, axis=0)
    parts = jnp.broadcast_to(part[None], (lax.axis_size("y"), PACKED, HEAD_DIM))
    parts = lax.all_to_all(parts, "y", split_axis=0, concat_axis=0, tiled=True)
    product, momentum_next = pl.pallas_call(
        newton_schulz,
        in_specs=[pl.BlockSpec(memory_space=pltpu.VMEM), pl.BlockSpec(memory_space=pl.ANY)],
        out_specs=[pl.BlockSpec(memory_space=pltpu.VMEM), pl.BlockSpec(memory_space=pl.ANY)],
        out_shape=[f32(PACKED, HEAD_DIM), f32(cols, rows)],
        scratch_shapes=[pltpu.SemaphoreType.DMA],
        compiler_params=pltpu.CompilerParams(vmem_limit_bytes=VMEM),
    )(parts, momentum_next)
    products = jnp.broadcast_to(product[None], (owners, PACKED, HEAD_DIM))
    products = lax.all_to_all(products, OWNERS, split_axis=0, concat_axis=0, tiled=True)
    update = pl.pallas_call(
        apply,
        in_specs=[pl.BlockSpec(memory_space=pltpu.VMEM)] * 2,
        out_specs=pl.BlockSpec(memory_space=pl.ANY),
        out_shape=f32(cols, rows),
        scratch_shapes=[pltpu.VMEM((cols, rows), jnp.float32), pltpu.SemaphoreType.DMA((heads,))],
        compiler_params=pltpu.CompilerParams(vmem_limit_bytes=VMEM),
    )(blended, products)
    return update, momentum_next


def solution(mesh):
    fine = Mesh(mesh.devices.reshape(8, 8, 4, 2), ("replica", *COLUMN_AXES))
    return jax.shard_map(
        on_device,
        mesh=fine,
        in_specs=(P("replica", COLUMN_AXES, None), P(COLUMN_AXES, "replica")),
        out_specs=(P(COLUMN_AXES, "replica"), P(COLUMN_AXES, "replica")),
        check_vma=False,
    )
```

```python
import functools
import math

import jax
import jax.numpy as jnp
from jax import lax
from jax.experimental import pallas as pl
from jax.experimental.pallas import tpu as pltpu
from jax.sharding import Mesh, PartitionSpec as P

COLS = 5120
HEAD_DIM = 128
HALF = HEAD_DIM // 2
PACKED = HALF + 8
ITERS = 5
VMEM = 32 * 1024 * 1024

quintic_a = 3.4445
quintic_b = -4.775
quintic_c = 2.0315
beta_decay = 0.95
norm_eps = 1e-07
highest = lax.Precision.HIGHEST

COLUMN_AXES = ("y", "x", "core")
OWNERS = ("x", "core")


def iotas(rows):
    shape = (rows, HEAD_DIM)
    return lax.broadcasted_iota(jnp.int32, shape, 0), lax.broadcasted_iota(jnp.int32, shape, 1)


def pack(full):
    i, j = iotas(HALF)
    body = jnp.where(j > i, full[:HALF], pltpu.roll(full[HALF:], HALF, 1))
    i, j = iotas(HEAD_DIM)
    diagonal = jnp.sum(jnp.where(i == j, full, 0.0), axis=0, keepdims=True)
    return body, jnp.broadcast_to(diagonal, (8, HEAD_DIM))


def unpack(packed):
    i, j = iotas(HALF)
    body = packed[:HALF]
    top = jnp.where(j > i, body, 0.0)
    bottom = pltpu.roll(jnp.where(j < i, body, 0.0), HALF, 1)
    triangle = jnp.concatenate([top, bottom], axis=0)
    i, j = iotas(HEAD_DIM)
    diagonal = jnp.broadcast_to(packed[HALF : HALF + 1], (HEAD_DIM, HEAD_DIM))
    return jnp.where(i == j, diagonal, triangle + triangle.T)


def dot(a, b, contract=((1,), (0,))):
    return lax.dot_general(
        a, b, (contract, ((), ())), precision=highest, preferred_element_type=jnp.float32
    )


def thirds(value):
    high = value.astype(jnp.bfloat16)
    rest = value - high.astype(jnp.float32)
    middle = rest.astype(jnp.bfloat16)
    return high, middle, (rest - middle.astype(jnp.float32)).astype(jnp.bfloat16)


def joined_dot(a, b):
    a0, a1, a2 = a
    b0, b1, b2 = b
    left = jnp.concatenate([a0, a1, a0, a2, a1, a0], axis=1)
    right = jnp.concatenate([b0, b0, b1, b0, b1, b2], axis=0)
    return lax.dot_general(left, right, (((1,), (0,)), ((), ())), preferred_element_type=jnp.float32)


def momentum_and_gram(*refs):
    *term_refs, momentum_ref, next_ref, blended_ref, gram_ref = refs
    grad_sum = term_refs[0][...]
    for term_ref in term_refs[1:]:
        grad_sum = grad_sum + term_ref[...]
    momentum_next = beta_decay * momentum_ref[...] + grad_sum
    next_ref[...] = momentum_next
    blended = grad_sum + beta_decay * momentum_next
    blended_ref[...] = blended
    heads = blended.shape[1] // HEAD_DIM
    cores = gram_ref.shape[0]
    for h in range(cores * gram_ref.shape[1]):
        core, x = h % cores, h // cores
        if h < heads:
            part = blended[:, h * HEAD_DIM : (h + 1) * HEAD_DIM]
            body, diagonal = pack(dot(part, part, ((0,), (0,))))
            gram_ref[core, x, :HALF] = body
            gram_ref[core, x, HALF:] = diagonal
        else:
            gram_ref[core, x] = jnp.zeros_like(gram_ref[core, x])


def newton_schulz(parts_ref, next_ref, out_ref, next_out_ref, sem):
    write = pltpu.make_async_copy(next_ref, next_out_ref, sem)
    write.start()
    packed = jnp.sum(parts_ref[...], axis=0)
    total = jnp.sum(packed[HALF : HALF + 1])
    scale = 1.0 / (jnp.sqrt(total) + norm_eps)
    square = unpack(packed) * scale * scale
    i, j = iotas(HEAD_DIM)
    eye = jnp.where(i == j, quintic_a, 0.0)
    product = None
    for iteration in range(ITERS):
        terms = thirds(square)
        polynomial = eye + quintic_b * square + quintic_c * joined_dot(terms, terms)
        factors = thirds(polynomial)
        product = polynomial if product is None else joined_dot(thirds(product), factors)
        if iteration < ITERS - 1:
            square = joined_dot(thirds(joined_dot(terms, factors)), factors)
            if iteration < 2:
                square = 0.5 * (square + square.T)
    factor = 0.2 * math.sqrt(max(HEAD_DIM, COLS))
    body, diagonal = pack(product * (factor * scale))
    out_ref[:HALF] = body
    out_ref[HALF:] = diagonal
    write.wait()


def apply(blended_ref, product_ref, out_ref, held, sems):
    writes = []
    for h in range(out_ref.shape[1] // HEAD_DIM):
        cols = slice(h * HEAD_DIM, (h + 1) * HEAD_DIM)
        held[:, cols] = dot(blended_ref[:, cols], unpack(product_ref[h]))
        writes.append(pltpu.make_async_copy(held.at[:, cols], out_ref.at[:, cols], sems.at[h]))
        writes[-1].start()
    for write in writes:
        write.wait()


def call(body, out_shape, *args):
    return pl.pallas_call(
        body,
        out_shape=out_shape,
        compiler_params=pltpu.CompilerParams(vmem_limit_bytes=VMEM),
    )(*args)


def f32(*shape):
    return jax.ShapeDtypeStruct(shape, jnp.float32)


def replica_sums(grad):
    size, me, core = lax.axis_size("replica"), lax.axis_index("replica"), lax.axis_index("core")
    width = grad.shape[1] // size
    toward = 1 - 2 * lax.rem(me + core, 2)

    def chunk(k):
        return lax.dynamic_slice(
            grad, (0, lax.rem(me + toward * k + size, size) * width), (grad.shape[0], width)
        )

    def send(value, distance):
        pairs = []
        for i in range(size):
            for c in range(2):
                j = (i + distance * (1 - 2 * ((i + c) % 2))) % size
                pairs.append((2 * i + c, 2 * j + c))
        return lax.ppermute(value, ("replica", "core"), pairs)

    offsets = (4, 3, 2, 1, -3, -2, -1, 0)
    chunks = dict(zip(offsets, lax.optimization_barrier(tuple(chunk(k) for k in offsets))))
    fourth, third, second = (send(chunks[k], 1) for k in (4, 3, 2))
    relayed = send(chunks[-3] + fourth, -2)
    to_second, chunks[1] = lax.optimization_barrier((chunks[-2] + third, chunks[1]))
    from_second = send(to_second, -2)
    partner = send(chunks[1], 1)
    from_first = send(chunks[-1] + second + relayed, -1)
    return chunks[0], partner, from_second, from_first


def on_device(grad_partials, momentum):
    terms = replica_sums(grad_partials[0])
    cols, rows = momentum.shape
    heads = rows // HEAD_DIM
    owners = lax.axis_size(OWNERS)
    owner_grid = (lax.axis_size("core"), lax.axis_size("x"))
    momentum_next, blended, gram = call(
        momentum_and_gram,
        (f32(cols, rows), f32(cols, rows), f32(*owner_grid, PACKED, HEAD_DIM)),
        *terms,
        momentum,
    )
    both = lax.all_gather(gram, "core")
    mine = lax.dynamic_index_in_dim(both, lax.axis_index("core"), axis=1, keepdims=False)
    parts = lax.all_to_all(jnp.sum(mine, axis=0), "x", split_axis=0, concat_axis=0, tiled=True)
    part = jnp.sum(parts, axis=0)
    parts = jnp.broadcast_to(part[None], (lax.axis_size("y"), PACKED, HEAD_DIM))
    parts = lax.all_to_all(parts, "y", split_axis=0, concat_axis=0, tiled=True)
    product, momentum_next = pl.pallas_call(
        newton_schulz,
        in_specs=[pl.BlockSpec(memory_space=pltpu.VMEM), pl.BlockSpec(memory_space=pl.ANY)],
        out_specs=[pl.BlockSpec(memory_space=pltpu.VMEM), pl.BlockSpec(memory_space=pl.ANY)],
        out_shape=[f32(PACKED, HEAD_DIM), f32(cols, rows)],
        scratch_shapes=[pltpu.SemaphoreType.DMA],
        compiler_params=pltpu.CompilerParams(vmem_limit_bytes=VMEM),
    )(parts, momentum_next)
    products = jnp.broadcast_to(product[None], (owners, PACKED, HEAD_DIM))
    products = lax.all_to_all(products, OWNERS, split_axis=0, concat_axis=0, tiled=True)
    update = pl.pallas_call(
        apply,
        in_specs=[pl.BlockSpec(memory_space=pltpu.VMEM)] * 2,
        out_specs=pl.BlockSpec(memory_space=pl.ANY),
        out_shape=f32(cols, rows),
        scratch_shapes=[pltpu.VMEM((cols, rows), jnp.float32), pltpu.SemaphoreType.DMA((heads,))],
        compiler_params=pltpu.CompilerParams(vmem_limit_bytes=VMEM),
    )(blended, products)
    return update, momentum_next


def solution(mesh):
    fine = Mesh(mesh.devices.reshape(8, 8, 4, 2), ("replica", *COLUMN_AXES))
    return jax.shard_map(
        on_device,
        mesh=fine,
        in_specs=(P("replica", COLUMN_AXES, None), P(COLUMN_AXES, "replica")),
        out_specs=(P(COLUMN_AXES, "replica"), P(COLUMN_AXES, "replica")),
        check_vma=False,
    )
```
